32 devices in a mesh: patch: 4 (over x, core), seq: 8 (over z, y).
Axes of the slice: x: 2, y: 2, z: 4, core: 2. Of those that a mesh axis runs over, the one named last changes fastest.
Arguments:
- fresh_qkv: bfloat16 [3, 576, 192, 128], P(None, ('patch', 'seq')), as said below
- stale_kv: bfloat16 [2, 576, 192, 128], P(None, None, 'seq'), may hold values from -6 to 6
- text_count: int32 [8], replicated, may hold values from 16 to 64
Outputs:
- attended: bfloat16 [576, 192, 128], P(('patch', 'seq'))
- refreshed_kv: bfloat16 [2, 576, 192, 128], P(None, None, 'seq')
The draws below stay inside these ranges and needn't reach their ends.
Inputs may be any that keep to these rules, and one draw needn't show every extreme that they name: `fresh_qkv`: each entry lies within -100 to 100.
All inputs are finite; a program needn't handle non-finite values.
Results may differ from the reference program's by a relative error of at most 0.0049.
Values may be sent and summed in bfloat16 or wider, within the bound.
A program may use at most 128 MiB of HBM per device.

```python
import math
import jax
import jax.numpy as jnp
from jax import lax

HEADS = 24
HDIM = 128
IMAGES = 8
TXT = 64
SEQ = 576
N_PATCH = 4


def draw_fresh_qkv(key, part):
    key = jax.random.fold_in(key, 11)
    key_base = jax.random.fold_in(key, 0)
    shape = (3, SEQ, IMAGES * HEADS, HDIM)
    base = jax.random.normal(key_base, shape, jnp.float32)
    return base.astype(jnp.bfloat16)


def set_ends(array, rng, least, high):
    shape = array.shape
    index_at = [jax.random.randint(jax.random.fold_in(rng, axis), (), 0, shape[axis]) for axis in range(len(shape))]
    array = array.at[tuple(index_at)].set(least)
    longest = shape.index(max(shape))
    index_at[longest] = (index_at[longest] + 1) % shape[longest]
    return array.at[tuple(index_at)].set(high)


def block_scale(rng, shape, cuts, low, high):
    level = 1.0
    for dim, parts in cuts:
        steps = jax.random.uniform(jax.random.fold_in(jax.random.fold_in(rng, 6), dim), (parts,), jnp.float32, low / len(cuts), high / len(cuts))
        level = level * jnp.repeat(jnp.exp(steps), shape[dim] // parts).reshape((-1,) + (1,) * (len(shape) - 1 - dim))
    return level


def normal_values(key, shape, width, limit, shards=(), dtype=jnp.bfloat16):
    entries = width * jax.random.normal(key, shape, jnp.float32)
    if shards:
        entries = entries * block_scale(key, shape, shards, -0.22, 0.18)
    return jnp.clip(entries, -limit, limit).astype(dtype)


def setup_inputs(seed: int = 0) -> dict:
    seeds = jax.random.split(jax.random.key(seed), 4)
    fresh_qkv = draw_fresh_qkv(jax.random.fold_in(seeds[3], 71), 0)
    stale_kv = normal_values(seeds[1], (2, SEQ, IMAGES * HEADS, HDIM), 1.0, 6.0, ((2, 8),))
    text_count = set_ends(jax.random.randint(seeds[2], (IMAGES,), TXT // 4, TXT + 1), jax.random.fold_in(seeds[2], 1), TXT // 4, TXT).astype(jnp.int32)
    return dict(fresh_qkv=fresh_qkv, stale_kv=stale_kv, text_count=text_count)


def reference(fresh_qkv, stale_kv, text_count):
    pair_count = fresh_qkv.shape[2]
    patch_len = SEQ // N_PATCH
    score_scale = 1.0 / math.sqrt(HDIM)
    fresh_pairs = jnp.transpose(fresh_qkv, (2, 0, 1, 3))
    stale_pairs = jnp.transpose(stale_kv, (2, 0, 1, 3))
    image_index = jnp.arange(pair_count) // HEADS
    valid_counts = text_count[image_index]
    position = jnp.arange(SEQ)

    def per_pair(operands):
        fresh_block, stale_block, valid_text = operands
        visible = (position >= TXT) | (position < valid_text)
        pieces = []
        for group in range(N_PATCH):
            start = group * patch_len
            key_block = stale_block[0].at[start:start + patch_len].set(fresh_block[1, start:start + patch_len])
            value_block = stale_block[1].at[start:start + patch_len].set(fresh_block[2, start:start + patch_len])
            query_rows = fresh_block[0, start:start + patch_len]
            scores = jnp.dot(query_rows, key_block.T, preferred_element_type=jnp.float32) * score_scale
            scores = jnp.where(visible[None, :], scores, -jnp.inf)
            highest = lax.optimization_barrier(jnp.max(scores, axis=1, keepdims=True))
            raised = jnp.exp(scores - highest)
            weights = (raised / lax.optimization_barrier(jnp.sum(raised, axis=1, keepdims=True))).astype(jnp.bfloat16)
            pieces.append(jnp.dot(weights, value_block, preferred_element_type=jnp.float32).astype(jnp.bfloat16))
        return jnp.concatenate(pieces, axis=0)
    outputs = jax.lax.map(per_pair, (fresh_pairs, stale_pairs, valid_counts))
    attended = jnp.transpose(outputs, (1, 0, 2))
    return (attended, fresh_qkv[1:3])
```

```python
import functools
import math

import jax
import jax.numpy as jnp
from jax import lax
from jax.experimental import pallas as pl
from jax.experimental.pallas import tpu as pltpu
from jax.sharding import PartitionSpec as P

HEADS = 24
TXT_DEV = 2
IMG_DEV = 16
PAIR_TILE = 8
MESH = pl.DeviceIdType.MESH


def fused_kernel(
    text_len,
    counts_ref,
    fresh_ref,
    stale_ref,
    attended_ref,
    refreshed_ref,
    recv,
    stale_vmem,
    wide,
    keys,
    values,
    queries,
    out_wide,
    out_send,
    in_send_sem,
    in_recv_sem,
    own_sem,
    stale_sem,
    fwd_send_sem,
    fwd_recv_sem,
    keep_sem,
    out_send_sem,
    out_recv_sem,
    out_own_sem,
):
    _, rows, peers, chunks, tile, hdim = fresh_ref.shape
    group_len = rows * peers
    seq_len = stale_ref.shape[1]
    p = lax.axis_index("patch")
    s = lax.axis_index("seq")
    core_twin = p + 1 - 2 * (p % 2)
    x_twin = (p + 2) % 4
    scale = 1.0 / math.sqrt(hdim)

    barrier = pltpu.get_barrier_semaphore()
    for step in range(1, peers):
        pl.semaphore_signal(
            barrier, inc=1, device_id=(p, (s + step) % peers), device_id_type=MESH
        )
    for twin in (core_twin, x_twin):
        pl.semaphore_signal(barrier, inc=1, device_id=(twin, s), device_id_type=MESH)

    stale_copies = []
    for c in range(chunks):
        for which in range(2):
            copy = pltpu.make_async_copy(
                stale_ref.at[which, :, c], stale_vmem.at[which, c], stale_sem.at[which, c]
            )
            copy.start()
            stale_copies.append(copy)
    own_copies = []
    for c in range(chunks):
        copy = pltpu.make_async_copy(
            fresh_ref.at[:, :, s, c], recv.at[c, :, pl.ds(rows * s, rows)], own_sem.at[c]
        )
        copy.start()
        own_copies.append(copy)
    pl.semaphore_wait(barrier, peers + 1)

    def in_copy(c, step):
        to = (s + step) % peers
        return pltpu.make_async_remote_copy(
            src_ref=fresh_ref.at[:, :, to, c],
            dst_ref=recv.at[c, :, pl.ds(rows * s, rows)],
            send_sem=in_send_sem.at[c, step],
            recv_sem=in_recv_sem.at[c, step],
            device_id=(p, to),
            device_id_type=MESH,
        )

    def in_arrival(c, step):
        origin = (s + peers - step) % peers
        return pltpu.make_async_remote_copy(
            src_ref=fresh_ref.at[:, :, origin, c],
            dst_ref=recv.at[c, :, pl.ds(rows * origin, rows)],
            send_sem=in_send_sem.at[c, step],
            recv_sem=in_recv_sem.at[c, step],
            device_id=(p, origin),
            device_id_type=MESH,
        )

    def forward(c, kind):
        if kind == 2:
            place = refreshed_ref.at[:, pl.ds(group_len * x_twin, group_len), c]
            source = place
        else:
            place = refreshed_ref.at[:, pl.ds(group_len * p, group_len), c]
            source = recv.at[c, pl.ds(1, 2)]
        return pltpu.make_async_remote_copy(
            src_ref=source,
            dst_ref=place,
            send_sem=fwd_send_sem.at[kind, c],
            recv_sem=fwd_recv_sem.at[kind, c],
            device_id=(x_twin if kind == 0 else core_twin, s),
            device_id_type=MESH,
        )

    def forward_arrival(c, kind):
        origin = {0: x_twin, 1: core_twin, 2: (core_twin + 2) % 4}[kind]
        return pltpu.make_async_remote_copy(
            src_ref=recv.at[c, pl.ds(1, 2)],
            dst_ref=refreshed_ref.at[:, pl.ds(group_len * origin, group_len), c],
            send_sem=fwd_send_sem.at[kind, c],
            recv_sem=fwd_recv_sem.at[kind, c],
            device_id=(x_twin if kind == 0 else core_twin, s),
            device_id_type=MESH,
        )

    def keep(c):
        return pltpu.make_async_copy(
            recv.at[c, pl.ds(1, 2)],
            refreshed_ref.at[:, pl.ds(group_len * p, group_len), c],
            keep_sem.at[c],
        )

    def out_copy(c, step):
        to = (s + step) % peers
        return pltpu.make_async_remote_copy(
            src_ref=out_send.at[c, pl.ds(rows * to, rows)],
            dst_ref=attended_ref.at[:, s, c],
            send_sem=out_send_sem.at[c, step],
            recv_sem=out_recv_sem.at[c, step],
            device_id=(p, to),
            device_id_type=MESH,
        )

    def out_arrival(c, step):
        origin = (s + peers - step) % peers
        return pltpu.make_async_remote_copy(
            src_ref=out_send.at[c, pl.ds(rows * origin, rows)],
            dst_ref=attended_ref.at[:, origin, c],
            send_sem=out_send_sem.at[c, step],
            recv_sem=out_recv_sem.at[c, step],
            device_id=(p, origin),
            device_id_type=MESH,
        )

    def out_own(c):
        return pltpu.make_async_copy(
            out_send.at[c, pl.ds(rows * s, rows)], attended_ref.at[:, s, c], out_own_sem.at[c]
        )

    for c in range(chunks):
        for step in range(1, peers):
            in_copy(c, step).start()

    for copy in stale_copies:
        copy.wait()
    for c in range(chunks):
        for which, target in ((0, keys), (1, values)):
            wide[...] = stale_vmem[which, c].astype(jnp.float32).reshape(seq_len * tile, hdim)
            for g in range(tile):
                target[c * tile + g] = wide[pl.ds(g, seq_len, stride=tile), :].astype(jnp.bfloat16)

    position = lax.broadcasted_iota(jnp.int32, (1, seq_len), 1)
    for c in range(chunks):
        own_copies[c].wait()
        for step in range(1, peers):
            in_arrival(c, step).wait_recv()
        forward(c, 0).start()
        forward(c, 1).start()
        keep(c).start()
        for which, target in ((0, queries), (1, keys), (2, values)):
            part = wide.at[pl.ds(0, group_len * tile)]
            part[...] = recv[c, which].astype(jnp.float32).reshape(group_len * tile, hdim)
            for g in range(tile):
                block = part[pl.ds(g, group_len, stride=tile), :].astype(jnp.bfloat16)
                if which == 0:
                    target[g] = block
                else:
                    target[c * tile + g, pl.ds(pl.multiple_of(group_len * p, 16), group_len), :] = block

        for g in range(tile):
            pair = c * tile + g
            scores = (
                lax.dot_general(
                    queries[g],
                    keys[pair],
                    (((1,), (1,)), ((), ())),
                    preferred_element_type=jnp.float32,
                )
                * scale
            )
            visible = (position >= text_len) | (position < counts_ref[pair])
            scores = jnp.where(visible, scores, -jnp.inf)
            highest = jnp.max(scores, axis=1, keepdims=True)
            raised = jnp.exp(scores - highest)
            weights = (raised / jnp.sum(raised, axis=1, keepdims=True)).astype(jnp.bfloat16)
            out_wide[pl.ds(g, group_len, stride=tile), :] = jnp.dot(
                weights, values[pair], preferred_element_type=jnp.float32
            )
        out_send[c] = out_wide[...].reshape(group_len, tile, hdim).astype(jnp.bfloat16)
        for step in range(1, peers):
            out_copy(c, step).start()
        out_own(c).start()
        if c:
            forward_arrival(c - 1, 0).wait_recv()
            forward(c - 1, 2).start()

    forward_arrival(chunks - 1, 0).wait_recv()
    forward(chunks - 1, 2).start()
    for c in range(chunks):
        for step in range(1, peers):
            in_copy(c, step).wait_send()
            out_copy(c, step).wait_send()
            out_arrival(c, step).wait_recv()
        out_own(c).wait()
        keep(c).wait()
        forward(c, 0).wait_send()
        for kind in (1, 2):
            forward(c, kind).wait_send()
            forward_arrival(c, kind).wait_recv()


def fused(fresh_qkv, stale_kv, valid_counts, text_len):
    peers = lax.axis_size("seq")
    _, rows, pair_count, hdim = fresh_qkv.shape
    pairs_here = pair_count // peers
    chunks = pairs_here // PAIR_TILE
    group_len = rows * peers
    seq_len = stale_kv.shape[1]
    bf16, f32 = jnp.bfloat16, jnp.float32
    fresh_blocks = fresh_qkv.reshape(3, rows, peers, chunks, PAIR_TILE, hdim)
    stale_blocks = stale_kv.reshape(2, seq_len, chunks, PAIR_TILE, hdim)
    dma = pltpu.SemaphoreType.DMA
    attended, refreshed = pl.pallas_call(
        functools.partial(fused_kernel, text_len),
        out_shape=(
            jax.ShapeDtypeStruct((rows, peers, chunks, PAIR_TILE, hdim), bf16),
            jax.ShapeDtypeStruct(stale_blocks.shape, bf16),
        ),
        in_specs=[
            pl.BlockSpec(memory_space=pltpu.SMEM),
            pl.BlockSpec(memory_space=pl.ANY),
            pl.BlockSpec(memory_space=pl.ANY),
        ],
        out_specs=(pl.BlockSpec(memory_space=pl.ANY), pl.BlockSpec(memory_space=pl.ANY)),
        scratch_shapes=[
            pltpu.VMEM((chunks, 3, group_len, PAIR_TILE, hdim), bf16),
            pltpu.VMEM((2, chunks, seq_len, PAIR_TILE, hdim), bf16),
            pltpu.VMEM((seq_len * PAIR_TILE, hdim), f32),
            pltpu.VMEM((pairs_here, seq_len, hdim), bf16),
            pltpu.VMEM((pairs_here, seq_len, hdim), bf16),
            pltpu.VMEM((PAIR_TILE, group_len, hdim), bf16),
            pltpu.VMEM((group_len * PAIR_TILE, hdim), f32),
            pltpu.VMEM((chunks, group_len, PAIR_TILE, hdim), bf16),
            dma((chunks, peers)),
            dma((chunks, peers)),
            dma((chunks,)),
            dma((2, chunks)),
            dma((3, chunks)),
            dma((3, chunks)),
            dma((chunks,)),
            dma((chunks, peers)),
            dma((chunks, peers)),
            dma((chunks,)),
        ],
        compiler_params=pltpu.CompilerParams(
            collective_id=0, has_side_effects=True, vmem_limit_bytes=48 * 1024 * 1024
        ),
        name="joint_attention",
    )(valid_counts, fresh_blocks, stale_blocks)
    return attended.reshape(rows, pair_count, hdim), refreshed.reshape(stale_kv.shape)


def attend(query_part, key_part, value_part, valid_counts, text_len):
    score_scale = 1.0 / math.sqrt(query_part.shape[-1])
    position = jnp.arange(key_part.shape[0])

    def per_pair(operands):
        query_rows, key_rows, value_rows, valid_text = operands
        scores = (
            lax.dot_general(
                query_rows, key_rows, (((1,), (1,)), ((), ())), preferred_element_type=jnp.float32
            )
            * score_scale
        )
        visible = (position >= text_len) | (position < valid_text)
        scores = jnp.where(visible[None, :], scores, -jnp.inf)
        highest = jnp.max(scores, axis=1, keepdims=True)
        raised = jnp.exp(scores - highest)
        weights = (raised / jnp.sum(raised, axis=1, keepdims=True)).astype(jnp.bfloat16)
        return jnp.dot(weights, value_rows, preferred_element_type=jnp.float32).astype(jnp.bfloat16)

    outputs = lax.map(
        per_pair,
        (
            jnp.moveaxis(query_part, 1, 0),
            jnp.moveaxis(key_part, 1, 0),
            jnp.moveaxis(value_part, 1, 0),
            valid_counts,
        ),
    )
    return jnp.moveaxis(outputs, 0, 1)


def per_device(fresh_qkv, stale_kv, text_count):
    seq_count = lax.axis_size("seq")
    shard_rows = fresh_qkv.shape[1]
    pairs_here = fresh_qkv.shape[2] // seq_count
    patch_len = shard_rows * seq_count
    patch_index = lax.axis_index("patch")
    first_pair = lax.axis_index("seq") * pairs_here
    seq_len = stale_kv.shape[1]
    text_len = TXT_DEV * seq_len // (TXT_DEV + IMG_DEV)
    image_index = (first_pair + jnp.arange(pairs_here)) // HEADS
    matches = image_index[:, None] == jnp.arange(text_count.shape[0])[None, :]
    valid_counts = jnp.sum(jnp.where(matches, text_count[None, :], 0), axis=1)
    if pairs_here % PAIR_TILE == 0 and patch_len % 16 == 0 and lax.axis_size("patch") == 4:
        return fused(fresh_qkv, stale_kv, valid_counts, text_len)
    exchanged = lax.all_to_all(fresh_qkv, "seq", split_axis=2, concat_axis=1, tiled=True)
    query_part = exchanged[0]
    own_kv = exchanged[1:]
    refreshed = lax.all_gather(own_kv, "patch", axis=1, tiled=True)
    merged_kv = lax.dynamic_update_slice_in_dim(stale_kv, own_kv, patch_index * patch_len, 1)
    attended_part = attend(query_part, merged_kv[0], merged_kv[1], valid_counts, text_len)
    result = lax.all_to_all(attended_part, "seq", split_axis=0, concat_axis=1, tiled=True)
    return (result, refreshed)


def solution(mesh):
    in_specs = (P(None, ("patch", "seq"), None, None), P(None, None, "seq", None), P())
    out_specs = (P(("patch", "seq"), None, None), P(None, None, "seq", None))
    return jax.shard_map(
        per_device, mesh=mesh, in_specs=in_specs, out_specs=out_specs, check_vma=False
    )
```

```python
import functools
import math

import jax
import jax.numpy as jnp
from jax import lax
from jax.experimental import pallas as pl
from jax.experimental.pallas import tpu as pltpu
from jax.sharding import PartitionSpec as P

HEADS = 24
TXT_DEV = 2
IMG_DEV = 16
PAIR_TILE = 8
MESH = pl.DeviceIdType.MESH


def fused_kernel(
    text_len,
    counts_ref,
    fresh_ref,
    stale_ref,
    attended_ref,
    refreshed_ref,
    counts,
    recv,
    stale_vmem,
    wide,
    keys,
    values,
    queries,
    out_wide,
    out_send,
    counts_sem,
    in_send_sem,
    in_recv_sem,
    own_sem,
    stale_sem,
    fwd_send_sem,
    fwd_recv_sem,
    keep_sem,
    out_send_sem,
    out_recv_sem,
    out_own_sem,
):
    _, rows, peers, chunks, tile, hdim = fresh_ref.shape
    group_len = rows * peers
    seq_len = stale_ref.shape[1]
    p = lax.axis_index("patch")
    s = lax.axis_index("seq")
    core_twin = p + 1 - 2 * (p % 2)
    x_twin = (p + 2) % 4
    scale = 1.0 / math.sqrt(hdim)

    barrier = pltpu.get_barrier_semaphore()
    for step in range(1, peers):
        pl.semaphore_signal(
            barrier, inc=1, device_id=(p, (s + step) % peers), device_id_type=MESH
        )
    for twin in (core_twin, x_twin):
        pl.semaphore_signal(barrier, inc=1, device_id=(twin, s), device_id_type=MESH)

    counts_copy = pltpu.make_async_copy(counts_ref, counts, counts_sem.at[0])
    counts_copy.start()
    stale_copies = []
    for c in range(chunks):
        for which in range(2):
            copy = pltpu.make_async_copy(
                stale_ref.at[which, :, c], stale_vmem.at[which, c], stale_sem.at[which, c]
            )
            copy.start()
            stale_copies.append(copy)
    own_copies = []
    for c in range(chunks):
        copy = pltpu.make_async_copy(
            fresh_ref.at[:, :, s, c], recv.at[c, :, pl.ds(rows * s, rows)], own_sem.at[c]
        )
        copy.start()
        own_copies.append(copy)
    pl.semaphore_wait(barrier, peers + 1)

    def in_copy(c, step):
        to = (s + step) % peers
        return pltpu.make_async_remote_copy(
            src_ref=fresh_ref.at[:, :, to, c],
            dst_ref=recv.at[c, :, pl.ds(rows * s, rows)],
            send_sem=in_send_sem.at[c, step],
            recv_sem=in_recv_sem.at[c, step],
            device_id=(p, to),
            device_id_type=MESH,
        )

    def in_arrival(c, step):
        origin = (s + peers - step) % peers
        return pltpu.make_async_remote_copy(
            src_ref=fresh_ref.at[:, :, origin, c],
            dst_ref=recv.at[c, :, pl.ds(rows * origin, rows)],
            send_sem=in_send_sem.at[c, step],
            recv_sem=in_recv_sem.at[c, step],
            device_id=(p, origin),
            device_id_type=MESH,
        )

    def forward(c, kind):
        if kind == 2:
            place = refreshed_ref.at[:, pl.ds(group_len * x_twin, group_len), c]
            source = place
        else:
            place = refreshed_ref.at[:, pl.ds(group_len * p, group_len), c]
            source = recv.at[c, pl.ds(1, 2)]
        return pltpu.make_async_remote_copy(
            src_ref=source,
            dst_ref=place,
            send_sem=fwd_send_sem.at[kind, c],
            recv_sem=fwd_recv_sem.at[kind, c],
            device_id=(x_twin if kind == 0 else core_twin, s),
            device_id_type=MESH,
        )

    def forward_arrival(c, kind):
        origin = {0: x_twin, 1: core_twin, 2: (core_twin + 2) % 4}[kind]
        return pltpu.make_async_remote_copy(
            src_ref=recv.at[c, pl.ds(1, 2)],
            dst_ref=refreshed_ref.at[:, pl.ds(group_len * origin, group_len), c],
            send_sem=fwd_send_sem.at[kind, c],
            recv_sem=fwd_recv_sem.at[kind, c],
            device_id=(x_twin if kind == 0 else core_twin, s),
            device_id_type=MESH,
        )

    def keep(c):
        return pltpu.make_async_copy(
            recv.at[c, pl.ds(1, 2)],
            refreshed_ref.at[:, pl.ds(group_len * p, group_len), c],
            keep_sem.at[c],
        )

    def out_copy(c, step):
        to = (s + step) % peers
        return pltpu.make_async_remote_copy(
            src_ref=out_send.at[c, pl.ds(rows * to, rows)],
            dst_ref=attended_ref.at[:, s, c],
            send_sem=out_send_sem.at[c, step],
            recv_sem=out_recv_sem.at[c, step],
            device_id=(p, to),
            device_id_type=MESH,
        )

    def out_arrival(c, step):
        origin = (s + peers - step) % peers
        return pltpu.make_async_remote_copy(
            src_ref=out_send.at[c, pl.ds(rows * origin, rows)],
            dst_ref=attended_ref.at[:, origin, c],
            send_sem=out_send_sem.at[c, step],
            recv_sem=out_recv_sem.at[c, step],
            device_id=(p, origin),
            device_id_type=MESH,
        )

    def out_own(c):
        return pltpu.make_async_copy(
            out_send.at[c, pl.ds(rows * s, rows)], attended_ref.at[:, s, c], out_own_sem.at[c]
        )

    def follow(c):
        for step in range(1, peers):
            in_copy(c, step).wait_send()
            if c + 1 < chunks:
                in_copy(c + 1, step).start()

    for step in range(1, peers):
        in_copy(0, step).start()

    counts_copy.wait()
    for copy in stale_copies:
        copy.wait()
    for c in range(chunks):
        for which, target in ((0, keys), (1, values)):
            wide[...] = stale_vmem[which, c].astype(jnp.float32).reshape(seq_len * tile, hdim)
            for g in range(tile):
                target[c * tile + g] = wide[pl.ds(g, seq_len, stride=tile), :].astype(jnp.bfloat16)

    position = lax.broadcasted_iota(jnp.int32, (1, seq_len), 1)
    for c in range(chunks):
        follow(c)
        own_copies[c].wait()
        for step in range(1, peers):
            in_arrival(c, step).wait_recv()
        forward(c, 0).start()
        forward(c, 1).start()
        keep(c).start()
        for which, target in ((0, queries), (1, keys), (2, values)):
            part = wide.at[pl.ds(0, group_len * tile)]
            part[...] = recv[c, which].astype(jnp.float32).reshape(group_len * tile, hdim)
            for g in range(tile):
                block = part[pl.ds(g, group_len, stride=tile), :].astype(jnp.bfloat16)
                if which == 0:
                    target[g] = block
                else:
                    target[c * tile + g, pl.ds(pl.multiple_of(group_len * p, 16), group_len), :] = block

        for g in range(tile):
            pair = c * tile + g
            scores = (
                lax.dot_general(
                    queries[g],
                    keys[pair],
                    (((1,), (1,)), ((), ())),
                    preferred_element_type=jnp.float32,
                )
                * scale
            )
            image = (s * (chunks * tile) + pair) // HEADS
            visible = (position >= text_len) | (position < counts[image])
            scores = jnp.where(visible, scores, -jnp.inf)
            highest = jnp.max(scores, axis=1, keepdims=True)
            raised = jnp.exp(scores - highest)
            weights = (raised / jnp.sum(raised, axis=1, keepdims=True)).astype(jnp.bfloat16)
            out_wide[pl.ds(g, group_len, stride=tile), :] = jnp.dot(
                weights, values[pair], preferred_element_type=jnp.float32
            )
        out_send[c] = out_wide[...].reshape(group_len, tile, hdim).astype(jnp.bfloat16)
        for step in range(1, peers):
            out_copy(c, step).start()
        out_own(c).start()
        if c:
            forward_arrival(c - 1, 0).wait_recv()
            forward(c - 1, 2).start()

    forward_arrival(chunks - 1, 0).wait_recv()
    forward(chunks - 1, 2).start()
    for c in range(chunks):
        for step in range(1, peers):
            out_copy(c, step).wait_send()
            out_arrival(c, step).wait_recv()
        out_own(c).wait()
        keep(c).wait()
        forward(c, 0).wait_send()
        for kind in (1, 2):
            forward(c, kind).wait_send()
            forward_arrival(c, kind).wait_recv()


def finish_kernel(attended_ref, refreshed_ref, attended_out, refreshed_out, sems):
    copies = [pltpu.make_async_copy(attended_ref, attended_out, sems.at[0, 0])]
    parts = 4
    length = refreshed_ref.shape[1] // parts
    for which in range(2):
        for part in range(parts):
            place = (which, pl.ds(part * length, length))
            copies.append(
                pltpu.make_async_copy(
                    refreshed_ref.at[place], refreshed_out.at[place], sems.at[1 + which, part]
                )
            )
    for copy in copies:
        copy.start()
    for copy in copies:
        copy.wait()


def fused(fresh_qkv, stale_kv, text_count, text_len):
    peers = lax.axis_size("seq")
    _, rows, pair_count, hdim = fresh_qkv.shape
    pairs_here = pair_count // peers
    chunks = pairs_here // PAIR_TILE
    group_len = rows * peers
    seq_len = stale_kv.shape[1]
    bf16, f32 = jnp.bfloat16, jnp.float32
    fresh_blocks = fresh_qkv.reshape(3, rows, peers, chunks, PAIR_TILE, hdim)
    stale_blocks = stale_kv.reshape(2, seq_len, chunks, PAIR_TILE, hdim)
    attended_shape = (rows, peers, chunks, PAIR_TILE, hdim)
    dma = pltpu.SemaphoreType.DMA
    in_hbm = pl.BlockSpec(memory_space=pltpu.HBM)
    anywhere = pl.BlockSpec(memory_space=pl.ANY)
    attended, refreshed = pl.pallas_call(
        functools.partial(fused_kernel, text_len),
        out_shape=(
            pltpu.VMEM(attended_shape, bf16),
            pltpu.VMEM(stale_blocks.shape, bf16),
        ),
        in_specs=[in_hbm, in_hbm, in_hbm],
        out_specs=(anywhere, anywhere),
        scratch_shapes=[
            pltpu.SMEM(text_count.shape, jnp.int32),
            pltpu.VMEM((chunks, 3, group_len, PAIR_TILE, hdim), bf16),
            pltpu.VMEM((2, chunks, seq_len, PAIR_TILE, hdim), bf16),
            pltpu.VMEM((seq_len * PAIR_TILE, hdim), f32),
            pltpu.VMEM((pairs_here, seq_len, hdim), bf16),
            pltpu.VMEM((pairs_here, seq_len, hdim), bf16),
            pltpu.VMEM((PAIR_TILE, group_len, hdim), bf16),
            pltpu.VMEM((group_len * PAIR_TILE, hdim), f32),
            pltpu.VMEM((chunks, group_len, PAIR_TILE, hdim), bf16),
            dma((1,)),
            dma((chunks, peers)),
            dma((chunks, peers)),
            dma((chunks,)),
            dma((2, chunks)),
            dma((3, chunks)),
            dma((3, chunks)),
            dma((chunks,)),
            dma((chunks, peers)),
            dma((chunks, peers)),
            dma((chunks,)),
        ],
        compiler_params=pltpu.CompilerParams(
            collective_id=0, has_side_effects=True, vmem_limit_bytes=32 * 1024 * 1024
        ),
        name="joint_attention",
    )(
        pltpu.with_memory_space_constraint(text_count, pltpu.HBM),
        pltpu.with_memory_space_constraint(fresh_blocks, pltpu.HBM),
        pltpu.with_memory_space_constraint(stale_blocks, pltpu.HBM),
    )
    attended, refreshed = pl.pallas_call(
        finish_kernel,
        out_shape=(
            jax.ShapeDtypeStruct(attended_shape, bf16),
            jax.ShapeDtypeStruct(stale_blocks.shape, bf16),
        ),
        in_specs=[anywhere, anywhere],
        out_specs=(in_hbm, in_hbm),
        scratch_shapes=[dma((3, 4))],
        name="results_to_hbm",
    )(attended, refreshed)
    return attended.reshape(rows, pair_count, hdim), refreshed.reshape(stale_kv.shape)


def attend(query_part, key_part, value_part, valid_counts, text_len):
    score_scale = 1.0 / math.sqrt(query_part.shape[-1])
    position = jnp.arange(key_part.shape[0])

    def per_pair(operands):
        query_rows, key_rows, value_rows, valid_text = operands
        scores = (
            lax.dot_general(
                query_rows, key_rows, (((1,), (1,)), ((), ())), preferred_element_type=jnp.float32
            )
            * score_scale
        )
        visible = (position >= text_len) | (position < valid_text)
        scores = jnp.where(visible[None, :], scores, -jnp.inf)
        highest = jnp.max(scores, axis=1, keepdims=True)
        raised = jnp.exp(scores - highest)
        weights = (raised / jnp.sum(raised, axis=1, keepdims=True)).astype(jnp.bfloat16)
        return jnp.dot(weights, value_rows, preferred_element_type=jnp.float32).astype(jnp.bfloat16)

    outputs = lax.map(
        per_pair,
        (
            jnp.moveaxis(query_part, 1, 0),
            jnp.moveaxis(key_part, 1, 0),
            jnp.moveaxis(value_part, 1, 0),
            valid_counts,
        ),
    )
    return jnp.moveaxis(outputs, 0, 1)


def per_device(fresh_qkv, stale_kv, text_count):
    seq_count = lax.axis_size("seq")
    shard_rows = fresh_qkv.shape[1]
    pairs_here = fresh_qkv.shape[2] // seq_count
    patch_len = shard_rows * seq_count
    patch_index = lax.axis_index("patch")
    first_pair = lax.axis_index("seq") * pairs_here
    seq_len = stale_kv.shape[1]
    text_len = TXT_DEV * seq_len // (TXT_DEV + IMG_DEV)
    image_index = (first_pair + jnp.arange(pairs_here)) // HEADS
    matches = image_index[:, None] == jnp.arange(text_count.shape[0])[None, :]
    valid_counts = jnp.sum(jnp.where(matches, text_count[None, :], 0), axis=1)
    if pairs_here % PAIR_TILE == 0 and patch_len % 16 == 0 and lax.axis_size("patch") == 4:
        return fused(fresh_qkv, stale_kv, text_count, text_len)
    exchanged = lax.all_to_all(fresh_qkv, "seq", split_axis=2, concat_axis=1, tiled=True)
    query_part = exchanged[0]
    own_kv = exchanged[1:]
    refreshed = lax.all_gather(own_kv, "patch", axis=1, tiled=True)
    merged_kv = lax.dynamic_update_slice_in_dim(stale_kv, own_kv, patch_index * patch_len, 1)
    attended_part = attend(query_part, merged_kv[0], merged_kv[1], valid_counts, text_len)
    result = lax.all_to_all(attended_part, "seq", split_axis=0, concat_axis=1, tiled=True)
    return (result, refreshed)


def solution(mesh):
    in_specs = (P(None, ("patch", "seq"), None, None), P(None, None, "seq", None), P())
    out_specs = (P(("patch", "seq"), None, None), P(None, None, "seq", None))
    return jax.shard_map(
        per_device, mesh=mesh, in_specs=in_specs, out_specs=out_specs, check_vma=False
    )
```

```python
import functools
import math

import jax
import jax.numpy as jnp
from jax import lax
from jax.experimental import pallas as pl
from jax.experimental.pallas import tpu as pltpu
from jax.sharding import PartitionSpec as P

HEADS = 24
TXT_DEV = 2
IMG_DEV = 16
PAIR_TILE = 8
MESH = pl.DeviceIdType.MESH


def fused_kernel(
    text_len,
    counts_ref,
    fresh_ref,
    stale_ref,
    attended_ref,
    refreshed_ref,
    counts,
    recv,
    stale_vmem,
    wide,
    keys,
    values,
    queries,
    out_wide,
    out_send,
    counts_sem,
    in_send_sem,
    in_recv_sem,
    own_sem,
    stale_sem,
    fwd_send_sem,
    fwd_recv_sem,
    keep_sem,
    out_send_sem,
    out_recv_sem,
    out_own_sem,
):
    _, rows, peers, chunks, tile, hdim = fresh_ref.shape
    group_len = rows * peers
    seq_len = stale_ref.shape[1]
    p = lax.axis_index("patch")
    s = lax.axis_index("seq")
    core_twin = p + 1 - 2 * (p % 2)
    x_twin = (p + 2) % 4
    scale = 1.0 / math.sqrt(hdim)

    barrier = pltpu.get_barrier_semaphore()
    for step in range(1, peers):
        pl.semaphore_signal(
            barrier, inc=1, device_id=(p, (s + step) % peers), device_id_type=MESH
        )
    for twin in (core_twin, x_twin):
        pl.semaphore_signal(barrier, inc=1, device_id=(twin, s), device_id_type=MESH)

    counts_copy = pltpu.make_async_copy(counts_ref, counts, counts_sem.at[0])
    counts_copy.start()
    stale_copies = []
    for c in range(chunks):
        for which in range(2):
            copy = pltpu.make_async_copy(
                stale_ref.at[which, :, c], stale_vmem.at[which, c], stale_sem.at[which, c]
            )
            copy.start()
            stale_copies.append(copy)
    own_copies = []
    for c in range(chunks):
        copy = pltpu.make_async_copy(
            fresh_ref.at[:, :, s, c], recv.at[c, :, pl.ds(rows * s, rows)], own_sem.at[c]
        )
        copy.start()
        own_copies.append(copy)
    pl.semaphore_wait(barrier, peers + 1)

    groups = [(0, 1, 2), (0, 0, 1)]
    groups += [(c, 1, 2) for c in range(1, chunks)]
    groups += [(c, 0, 1) for c in range(1, chunks)]

    def in_copy(k, step):
        c, first, count = groups[k]
        to = (s + step) % peers
        return pltpu.make_async_remote_copy(
            src_ref=fresh_ref.at[pl.ds(first, count), :, to, c],
            dst_ref=recv.at[c, pl.ds(first, count), pl.ds(rows * s, rows)],
            send_sem=in_send_sem.at[k, step],
            recv_sem=in_recv_sem.at[k, step],
            device_id=(p, to),
            device_id_type=MESH,
        )

    def in_arrival(k, step):
        c, first, count = groups[k]
        origin = (s + peers - step) % peers
        return pltpu.make_async_remote_copy(
            src_ref=fresh_ref.at[pl.ds(first, count), :, origin, c],
            dst_ref=recv.at[c, pl.ds(first, count), pl.ds(rows * origin, rows)],
            send_sem=in_send_sem.at[k, step],
            recv_sem=in_recv_sem.at[k, step],
            device_id=(p, origin),
            device_id_type=MESH,
        )

    def forward(c, kind):
        if kind == 2:
            place = refreshed_ref.at[:, pl.ds(group_len * x_twin, group_len), c]
            source = place
        else:
            place = refreshed_ref.at[:, pl.ds(group_len * p, group_len), c]
            source = recv.at[c, pl.ds(1, 2)]
        return pltpu.make_async_remote_copy(
            src_ref=source,
            dst_ref=place,
            send_sem=fwd_send_sem.at[kind, c],
            recv_sem=fwd_recv_sem.at[kind, c],
            device_id=(x_twin if kind == 0 else core_twin, s),
            device_id_type=MESH,
        )

    def forward_arrival(c, kind):
        origin = {0: x_twin, 1: core_twin, 2: (core_twin + 2) % 4}[kind]
        return pltpu.make_async_remote_copy(
            src_ref=recv.at[c, pl.ds(1, 2)],
            dst_ref=refreshed_ref.at[:, pl.ds(group_len * origin, group_len), c],
            send_sem=fwd_send_sem.at[kind, c],
            recv_sem=fwd_recv_sem.at[kind, c],
            device_id=(x_twin if kind == 0 else core_twin, s),
            device_id_type=MESH,
        )

    def keep(c):
        return pltpu.make_async_copy(
            recv.at[c, pl.ds(1, 2)],
            refreshed_ref.at[:, pl.ds(group_len * p, group_len), c],
            keep_sem.at[c],
        )

    def out_copy(c, step):
        to = (s + step) % peers
        return pltpu.make_async_remote_copy(
            src_ref=out_send.at[c, pl.ds(rows * to, rows)],
            dst_ref=attended_ref.at[:, s, c],
            send_sem=out_send_sem.at[c, step],
            recv_sem=out_recv_sem.at[c, step],
            device_id=(p, to),
            device_id_type=MESH,
        )

    def out_arrival(c, step):
        origin = (s + peers - step) % peers
        return pltpu.make_async_remote_copy(
            src_ref=out_send.at[c, pl.ds(rows * origin, rows)],
            dst_ref=attended_ref.at[:, origin, c],
            send_sem=out_send_sem.at[c, step],
            recv_sem=out_recv_sem.at[c, step],
            device_id=(p, origin),
            device_id_type=MESH,
        )

    def out_own(c):
        return pltpu.make_async_copy(
            out_send.at[c, pl.ds(rows * s, rows)], attended_ref.at[:, s, c], out_own_sem.at[c]
        )

    def follow(k):
        for step in range(1, peers):
            in_copy(k, step).wait_send()
            if k + 2 < len(groups):
                in_copy(k + 2, step).start()

    for k in range(2):
        for step in range(1, peers):
            in_copy(k, step).start()

    counts_copy.wait()
    for copy in stale_copies:
        copy.wait()
    for c in range(chunks):
        for which, target in ((0, keys), (1, values)):
            wide[...] = stale_vmem[which, c].astype(jnp.float32).reshape(seq_len * tile, hdim)
            for g in range(tile):
                target[c * tile + g] = wide[pl.ds(g, seq_len, stride=tile), :].astype(jnp.bfloat16)

    masked_lanes = min(seq_len, -(-text_len // 128) * 128)
    position = lax.broadcasted_iota(jnp.int32, (1, masked_lanes), 1)

    def rows_of_pairs(c, which):
        part = wide.at[pl.ds(0, group_len * tile)]
        part[...] = recv[c, which].astype(jnp.float32).reshape(group_len * tile, hdim)
        return [
            part[pl.ds(g, group_len, stride=tile), :].astype(jnp.bfloat16) for g in range(tile)
        ]

    def take_keys(c):
        forward(c, 0).start()
        forward(c, 1).start()
        keep(c).start()
        place = pl.ds(pl.multiple_of(group_len * p, 16), group_len)
        for which, target in ((1, keys), (2, values)):
            for g, block in enumerate(rows_of_pairs(c, which)):
                target[c * tile + g, place, :] = block

    def attend_chunk(c):
        for g, query in enumerate(rows_of_pairs(c, 0)):
            queries[g] = query
        for g in range(tile):
            pair = c * tile + g
            scores = lax.dot_general(
                queries[g], keys[pair], (((1,), (1,)), ((), ())), preferred_element_type=jnp.float32
            )
            image = (s * (chunks * tile) + pair) // HEADS
            visible = (position >= text_len) | (position < counts[image])
            text_scores = jnp.where(visible, scores[:, :masked_lanes], -jnp.inf)
            if masked_lanes < seq_len:
                scores = jnp.concatenate([text_scores, scores[:, masked_lanes:]], axis=1)
            else:
                scores = text_scores
            highest = jnp.max(scores, axis=1, keepdims=True)
            raised = jnp.exp2((scores - highest) * (scale * math.log2(math.e)))
            total = jnp.sum(raised, axis=1, keepdims=True)
            weights = (raised * (1.0 / total)).astype(jnp.bfloat16)
            out_wide[pl.ds(g, group_len, stride=tile), :] = jnp.dot(
                weights, values[pair], preferred_element_type=jnp.float32
            )
        out_send[c] = out_wide[...].reshape(group_len, tile, hdim).astype(jnp.bfloat16)
        for step in range(1, peers):
            out_copy(c, step).start()
        out_own(c).start()

    relays = 0
    for copy in own_copies:
        copy.wait()
    for k, (c, first, _) in enumerate(groups):
        follow(k)
        for step in range(1, peers):
            in_arrival(k, step).wait_recv()
        if first == 1:
            take_keys(c)
        else:
            attend_chunk(c)
        if k >= 2 and relays + 1 < chunks:
            forward_arrival(relays, 0).wait_recv()
            forward(relays, 2).start()
            relays += 1

    forward_arrival(chunks - 1, 0).wait_recv()
    forward(chunks - 1, 2).start()
    for c in range(chunks):
        for step in range(1, peers):
            out_copy(c, step).wait_send()
            out_arrival(c, step).wait_recv()
        out_own(c).wait()
        keep(c).wait()
        forward(c, 0).wait_send()
        for kind in (1, 2):
            forward(c, kind).wait_send()
            forward_arrival(c, kind).wait_recv()


def fused(fresh_qkv, stale_kv, text_count, text_len):
    peers = lax.axis_size("seq")
    _, rows, pair_count, hdim = fresh_qkv.shape
    pairs_here = pair_count // peers
    chunks = pairs_here // PAIR_TILE
    group_len = rows * peers
    seq_len = stale_kv.shape[1]
    bf16, f32 = jnp.bfloat16, jnp.float32
    fresh_blocks = fresh_qkv.reshape(3, rows, peers, chunks, PAIR_TILE, hdim)
    stale_blocks = stale_kv.reshape(2, seq_len, chunks, PAIR_TILE, hdim)
    attended_shape = (rows, peers, chunks, PAIR_TILE, hdim)
    dma = pltpu.SemaphoreType.DMA
    in_hbm = pl.BlockSpec(memory_space=pltpu.HBM)
    anywhere = pl.BlockSpec(memory_space=pl.ANY)
    attended, refreshed = pl.pallas_call(
        functools.partial(fused_kernel, text_len),
        out_shape=(
            pltpu.VMEM(attended_shape, bf16),
            pltpu.VMEM(stale_blocks.shape, bf16),
        ),
        in_specs=[in_hbm, in_hbm, in_hbm],
        out_specs=(anywhere, anywhere),
        scratch_shapes=[
            pltpu.SMEM(text_count.shape, jnp.int32),
            pltpu.VMEM((chunks, 3, group_len, PAIR_TILE, hdim), bf16),
            pltpu.VMEM((2, chunks, seq_len, PAIR_TILE, hdim), bf16),
            pltpu.VMEM((seq_len * PAIR_TILE, hdim), f32),
            pltpu.VMEM((pairs_here, seq_len, hdim), bf16),
            pltpu.VMEM((pairs_here, seq_len, hdim), bf16),
            pltpu.VMEM((PAIR_TILE, group_len, hdim), bf16),
            pltpu.VMEM((group_len * PAIR_TILE, hdim), f32),
            pltpu.VMEM((chunks, group_len, PAIR_TILE, hdim), bf16),
            dma((1,)),
            dma((2 * chunks, peers)),
            dma((2 * chunks, peers)),
            dma((chunks,)),
            dma((2, chunks)),
            dma((3, chunks)),
            dma((3, chunks)),
            dma((chunks,)),
            dma((chunks, peers)),
            dma((chunks, peers)),
            dma((chunks,)),
        ],
        compiler_params=pltpu.CompilerParams(
            collective_id=0, has_side_effects=True, vmem_limit_bytes=32 * 1024 * 1024
        ),
        name="joint_attention",
    )(
        pltpu.with_memory_space_constraint(text_count, pltpu.HBM),
        pltpu.with_memory_space_constraint(fresh_blocks, pltpu.HBM),
        pltpu.with_memory_space_constraint(stale_blocks, pltpu.HBM),
    )
    return attended.reshape(rows, pair_count, hdim), refreshed.reshape(stale_kv.shape)


def attend(query_part, key_part, value_part, valid_counts, text_len):
    score_scale = 1.0 / math.sqrt(query_part.shape[-1])
    position = jnp.arange(key_part.shape[0])

    def per_pair(operands):
        query_rows, key_rows, value_rows, valid_text = operands
        scores = (
            lax.dot_general(
                query_rows, key_rows, (((1,), (1,)), ((), ())), preferred_element_type=jnp.float32
            )
            * score_scale
        )
        visible = (position >= text_len) | (position < valid_text)
        scores = jnp.where(visible[None, :], scores, -jnp.inf)
        highest = jnp.max(scores, axis=1, keepdims=True)
        raised = jnp.exp(scores - highest)
        weights = (raised / jnp.sum(raised, axis=1, keepdims=True)).astype(jnp.bfloat16)
        return jnp.dot(weights, value_rows, preferred_element_type=jnp.float32).astype(jnp.bfloat16)

    outputs = lax.map(
        per_pair,
        (
            jnp.moveaxis(query_part, 1, 0),
            jnp.moveaxis(key_part, 1, 0),
            jnp.moveaxis(value_part, 1, 0),
            valid_counts,
        ),
    )
    return jnp.moveaxis(outputs, 0, 1)


def per_device(fresh_qkv, stale_kv, text_count):
    seq_count = lax.axis_size("seq")
    shard_rows = fresh_qkv.shape[1]
    pairs_here = fresh_qkv.shape[2] // seq_count
    patch_len = shard_rows * seq_count
    patch_index = lax.axis_index("patch")
    first_pair = lax.axis_index("seq") * pairs_here
    seq_len = stale_kv.shape[1]
    text_len = TXT_DEV * seq_len // (TXT_DEV + IMG_DEV)
    image_index = (first_pair + jnp.arange(pairs_here)) // HEADS
    matches = image_index[:, None] == jnp.arange(text_count.shape[0])[None, :]
    valid_counts = jnp.sum(jnp.where(matches, text_count[None, :], 0), axis=1)
    if pairs_here % PAIR_TILE == 0 and patch_len % 16 == 0 and lax.axis_size("patch") == 4:
        return fused(fresh_qkv, stale_kv, text_count, text_len)
    exchanged = lax.all_to_all(fresh_qkv, "seq", split_axis=2, concat_axis=1, tiled=True)
    query_part = exchanged[0]
    own_kv = exchanged[1:]
    refreshed = lax.all_gather(own_kv, "patch", axis=1, tiled=True)
    merged_kv = lax.dynamic_update_slice_in_dim(stale_kv, own_kv, patch_index * patch_len, 1)
    attended_part = attend(query_part, merged_kv[0], merged_kv[1], valid_counts, text_len)
    result = lax.all_to_all(attended_part, "seq", split_axis=0, concat_axis=1, tiled=True)
    return (result, refreshed)


def solution(mesh):
    in_specs = (P(None, ("patch", "seq"), None, None), P(None, None, "seq", None), P())
    out_specs = (P(("patch", "seq"), None, None), P(None, None, "seq", None))
    return jax.shard_map(
        per_device, mesh=mesh, in_specs=in_specs, out_specs=out_specs, check_vma=False
    )
```

```python
import functools
import math

import jax
import jax.numpy as jnp
from jax import lax
from jax.experimental import pallas as pl
from jax.experimental.pallas import tpu as pltpu
from jax.sharding import PartitionSpec as P

HEADS = 24
TXT_DEV = 2
IMG_DEV = 16
PAIR_TILE = 8
MESH = pl.DeviceIdType.MESH


def fused_kernel(
    text_len,
    counts_ref,
    fresh_ref,
    stale_ref,
    attended_ref,
    refreshed_ref,
    counts,
    recv,
    stale_vmem,
    wide,
    keys,
    values,
    queries,
    out_wide,
    out_send,
    counts_sem,
    in_send_sem,
    in_recv_sem,
    own_sem,
    stale_sem,
    fwd_send_sem,
    fwd_recv_sem,
    keep_sem,
    out_send_sem,
    out_recv_sem,
    out_own_sem,
):
    _, rows, peers, chunks, tile, hdim = fresh_ref.shape
    group_len = rows * peers
    seq_len = stale_ref.shape[1]
    p = lax.axis_index("patch")
    s = lax.axis_index("seq")
    core_twin = p + 1 - 2 * (p % 2)
    x_twin = (p + 2) % 4
    scale = 1.0 / math.sqrt(hdim)

    barrier = pltpu.get_barrier_semaphore()
    for step in range(1, peers):
        pl.semaphore_signal(
            barrier, inc=1, device_id=(p, (s + step) % peers), device_id_type=MESH
        )
    for twin in (core_twin, x_twin):
        pl.semaphore_signal(barrier, inc=1, device_id=(twin, s), device_id_type=MESH)

    pl.semaphore_wait(barrier, peers + 1)

    groups = [(0, 1, 2), (0, 0, 1)]
    groups += [(c, 1, 2) for c in range(1, chunks)]
    groups += [(c, 0, 1) for c in range(1, chunks)]

    def in_copy(k, step):
        c, first, count = groups[k]
        to = (s + step) % peers
        return pltpu.make_async_remote_copy(
            src_ref=fresh_ref.at[pl.ds(first, count), :, to, c],
            dst_ref=recv.at[c, pl.ds(first, count), pl.ds(rows * s, rows)],
            send_sem=in_send_sem.at[k, step],
            recv_sem=in_recv_sem.at[k, step],
            device_id=(p, to),
            device_id_type=MESH,
        )

    def in_arrival(k, step):
        c, first, count = groups[k]
        origin = (s + peers - step) % peers
        return pltpu.make_async_remote_copy(
            src_ref=fresh_ref.at[pl.ds(first, count), :, origin, c],
            dst_ref=recv.at[c, pl.ds(first, count), pl.ds(rows * origin, rows)],
            send_sem=in_send_sem.at[k, step],
            recv_sem=in_recv_sem.at[k, step],
            device_id=(p, origin),
            device_id_type=MESH,
        )

    def forward(c, kind):
        if kind == 2:
            place = refreshed_ref.at[:, pl.ds(group_len * x_twin, group_len), c]
            source = place
        else:
            place = refreshed_ref.at[:, pl.ds(group_len * p, group_len), c]
            source = recv.at[c, pl.ds(1, 2)]
        return pltpu.make_async_remote_copy(
            src_ref=source,
            dst_ref=place,
            send_sem=fwd_send_sem.at[kind, c],
            recv_sem=fwd_recv_sem.at[kind, c],
            device_id=(x_twin if kind == 0 else core_twin, s),
            device_id_type=MESH,
        )

    def forward_arrival(c, kind):
        origin = {0: x_twin, 1: core_twin, 2: (core_twin + 2) % 4}[kind]
        return pltpu.make_async_remote_copy(
            src_ref=recv.at[c, pl.ds(1, 2)],
            dst_ref=refreshed_ref.at[:, pl.ds(group_len * origin, group_len), c],
            send_sem=fwd_send_sem.at[kind, c],
            recv_sem=fwd_recv_sem.at[kind, c],
            device_id=(x_twin if kind == 0 else core_twin, s),
            device_id_type=MESH,
        )

    def keep(c):
        return pltpu.make_async_copy(
            recv.at[c, pl.ds(1, 2)],
            refreshed_ref.at[:, pl.ds(group_len * p, group_len), c],
            keep_sem.at[c],
        )

    half = peers // 2
    near = s // half

    def out_peer(c, slot, sign):
        if c + 1 < chunks:
            return (s + peers + sign * slot) % peers
        if slot < half:
            return near * half + (s % half + half + sign * slot) % half
        return (1 - near) * half + (s % half + half + sign * (slot - half)) % half

    def out_copy(c, slot):
        to = out_peer(c, slot, 1)
        return pltpu.make_async_remote_copy(
            src_ref=out_send.at[c, pl.ds(rows * to, rows)],
            dst_ref=attended_ref.at[:, s, c],
            send_sem=out_send_sem.at[c, slot],
            recv_sem=out_recv_sem.at[c, slot],
            device_id=(p, to),
            device_id_type=MESH,
        )

    def out_arrival(c, slot):
        origin = out_peer(c, slot, -1)
        return pltpu.make_async_remote_copy(
            src_ref=out_send.at[c, pl.ds(rows * origin, rows)],
            dst_ref=attended_ref.at[:, origin, c],
            send_sem=out_send_sem.at[c, slot],
            recv_sem=out_recv_sem.at[c, slot],
            device_id=(p, origin),
            device_id_type=MESH,
        )

    def out_own(c):
        return pltpu.make_async_copy(
            out_send.at[c, pl.ds(rows * s, rows)], attended_ref.at[:, s, c], out_own_sem.at[c]
        )

    flight = 3

    def follow(k):
        for step in range(1, peers):
            in_copy(k, step).wait_send()
            if k + flight < len(groups):
                in_copy(k + flight, step).start()

    for step in range(1, peers):
        in_copy(0, step).start()
    counts_copy = pltpu.make_async_copy(counts_ref, counts, counts_sem.at[0])
    counts_copy.start()
    stale_copies = []
    for c in range(chunks):
        for which in range(2):
            copy = pltpu.make_async_copy(
                stale_ref.at[which, :, c], stale_vmem.at[which, c], stale_sem.at[which, c]
            )
            copy.start()
            stale_copies.append(copy)
    own_copies = []
    for c in range(chunks):
        copy = pltpu.make_async_copy(
            fresh_ref.at[:, :, s, c], recv.at[c, :, pl.ds(rows * s, rows)], own_sem.at[c]
        )
        copy.start()
        own_copies.append(copy)
    for k in range(1, min(flight, len(groups))):
        for step in range(1, peers):
            in_copy(k, step).start()

    counts_copy.wait()
    for copy in stale_copies:
        copy.wait()
    for c in range(chunks):
        for which, target in ((0, keys), (1, values)):
            wide[...] = stale_vmem[which, c].astype(jnp.float32).reshape(seq_len * tile, hdim)
            for g in range(tile):
                target[c * tile + g] = wide[pl.ds(g, seq_len, stride=tile), :].astype(jnp.bfloat16)

    masked_lanes = min(seq_len, -(-text_len // 128) * 128)
    position = lax.broadcasted_iota(jnp.int32, (1, masked_lanes), 1)

    def rows_of_pairs(c, which, start=0, count=group_len):
        part = wide.at[pl.ds(0, count * tile)]
        block = recv[c, which, pl.ds(start, count)]
        part[...] = block.astype(jnp.float32).reshape(count * tile, hdim)
        return [part[pl.ds(g, count, stride=tile), :].astype(jnp.bfloat16) for g in range(tile)]

    def take_keys(c):
        forward(c, 0).start()
        forward(c, 1).start()
        keep(c).start()
        place = pl.ds(pl.multiple_of(group_len * p, 16), group_len)
        for which, target in ((1, keys), (2, values)):
            for g, block in enumerate(rows_of_pairs(c, which)):
                target[c * tile + g, place, :] = block

    def attend_rows(c, start, count):
        for g, query in enumerate(rows_of_pairs(c, 0, start, count)):
            queries[g, :count] = query
        for g in range(tile):
            pair = c * tile + g
            scores = lax.dot_general(
                queries[g, :count], keys[pair], (((1,), (1,)), ((), ())), preferred_element_type=jnp.float32
            )
            image = (s * (chunks * tile) + pair) // HEADS
            visible = (position >= text_len) | (position < counts[image])
            text_scores = jnp.where(visible, scores[:, :masked_lanes], -jnp.inf)
            if masked_lanes < seq_len:
                scores = jnp.concatenate([text_scores, scores[:, masked_lanes:]], axis=1)
            else:
                scores = text_scores
            highest = jnp.max(scores, axis=1, keepdims=True)
            raised = jnp.exp2((scores - highest) * (scale * math.log2(math.e)))
            total = jnp.sum(raised, axis=1, keepdims=True)
            weights = (raised * (1.0 / total)).astype(jnp.bfloat16)
            out_wide[pl.ds(g, count, stride=tile), :] = jnp.dot(
                weights, values[pair], preferred_element_type=jnp.float32
            )
        block = out_wide[: count * tile].reshape(count, tile, hdim).astype(jnp.bfloat16)
        out_send[c, pl.ds(start, count)] = block

    def relay(c):
        forward_arrival(c, 0).wait_recv()
        forward(c, 2).start()

    def attend_chunk(c):
        if c + 1 < chunks:
            attend_rows(c, 0, group_len)
            for slot in range(1, peers):
                out_copy(c, slot).start()
        else:
            attend_rows(c, (1 - near) * (rows * half), rows * half)
            for slot in range(half, peers):
                out_copy(c, slot).start()
            relay(c)
            attend_rows(c, near * (rows * half), rows * half)
            for slot in range(1, half):
                out_copy(c, slot).start()
        out_own(c).start()

    relays = 0
    for copy in own_copies:
        copy.wait()
    for k, (c, first, _) in enumerate(groups):
        follow(k)
        for step in range(1, peers):
            in_arrival(k, step).wait_recv()
        if first == 1:
            take_keys(c)
        else:
            attend_chunk(c)
        if k >= 2 and relays + 1 < chunks:
            relay(relays)
            relays += 1

    for c in range(chunks):
        for step in range(1, peers):
            out_copy(c, step).wait_send()
            out_arrival(c, step).wait_recv()
        out_own(c).wait()
        keep(c).wait()
        forward(c, 0).wait_send()
        for kind in (1, 2):
            forward(c, kind).wait_send()
            forward_arrival(c, kind).wait_recv()


def fused(fresh_qkv, stale_kv, text_count, text_len):
    peers = lax.axis_size("seq")
    _, rows, pair_count, hdim = fresh_qkv.shape
    pairs_here = pair_count // peers
    chunks = pairs_here // PAIR_TILE
    group_len = rows * peers
    seq_len = stale_kv.shape[1]
    bf16, f32 = jnp.bfloat16, jnp.float32
    fresh_blocks = fresh_qkv.reshape(3, rows, peers, chunks, PAIR_TILE, hdim)
    stale_blocks = stale_kv.reshape(2, seq_len, chunks, PAIR_TILE, hdim)
    attended_shape = (rows, peers, chunks, PAIR_TILE, hdim)
    dma = pltpu.SemaphoreType.DMA
    in_hbm = pl.BlockSpec(memory_space=pltpu.HBM)
    anywhere = pl.BlockSpec(memory_space=pl.ANY)
    attended, refreshed = pl.pallas_call(
        functools.partial(fused_kernel, text_len),
        out_shape=(
            pltpu.VMEM(attended_shape, bf16),
            pltpu.VMEM(stale_blocks.shape, bf16),
        ),
        in_specs=[in_hbm, in_hbm, in_hbm],
        out_specs=(anywhere, anywhere),
        scratch_shapes=[
            pltpu.SMEM(text_count.shape, jnp.int32),
            pltpu.VMEM((chunks, 3, group_len, PAIR_TILE, hdim), bf16),
            pltpu.VMEM((2, chunks, seq_len, PAIR_TILE, hdim), bf16),
            pltpu.VMEM((seq_len * PAIR_TILE, hdim), f32),
            pltpu.VMEM((pairs_here, seq_len, hdim), bf16),
            pltpu.VMEM((pairs_here, seq_len, hdim), bf16),
            pltpu.VMEM((PAIR_TILE, group_len, hdim), bf16),
            pltpu.VMEM((group_len * PAIR_TILE, hdim), f32),
            pltpu.VMEM((chunks, group_len, PAIR_TILE, hdim), bf16),
            dma((1,)),
            dma((2 * chunks, peers)),
            dma((2 * chunks, peers)),
            dma((chunks,)),
            dma((2, chunks)),
            dma((3, chunks)),
            dma((3, chunks)),
            dma((chunks,)),
            dma((chunks, peers)),
            dma((chunks, peers)),
            dma((chunks,)),
        ],
        compiler_params=pltpu.CompilerParams(
            collective_id=0, has_side_effects=True, vmem_limit_bytes=32 * 1024 * 1024
        ),
        name="joint_attention",
    )(
        pltpu.with_memory_space_constraint(text_count, pltpu.HBM),
        pltpu.with_memory_space_constraint(fresh_blocks, pltpu.HBM),
        pltpu.with_memory_space_constraint(stale_blocks, pltpu.HBM),
    )
    return attended.reshape(rows, pair_count, hdim), refreshed.reshape(stale_kv.shape)


def attend(query_part, key_part, value_part, valid_counts, text_len):
    score_scale = 1.0 / math.sqrt(query_part.shape[-1])
    position = jnp.arange(key_part.shape[0])

    def per_pair(operands):
        query_rows, key_rows, value_rows, valid_text = operands
        scores = (
            lax.dot_general(
                query_rows, key_rows, (((1,), (1,)), ((), ())), preferred_element_type=jnp.float32
            )
            * score_scale
        )
        visible = (position >= text_len) | (position < valid_text)
        scores = jnp.where(visible[None, :], scores, -jnp.inf)
        highest = jnp.max(scores, axis=1, keepdims=True)
        raised = jnp.exp(scores - highest)
        weights = (raised / jnp.sum(raised, axis=1, keepdims=True)).astype(jnp.bfloat16)
        return jnp.dot(weights, value_rows, preferred_element_type=jnp.float32).astype(jnp.bfloat16)

    outputs = lax.map(
        per_pair,
        (
            jnp.moveaxis(query_part, 1, 0),
            jnp.moveaxis(key_part, 1, 0),
            jnp.moveaxis(value_part, 1, 0),
            valid_counts,
        ),
    )
    return jnp.moveaxis(outputs, 0, 1)


def per_device(fresh_qkv, stale_kv, text_count):
    seq_count = lax.axis_size("seq")
    shard_rows = fresh_qkv.shape[1]
    pairs_here = fresh_qkv.shape[2] // seq_count
    patch_len = shard_rows * seq_count
    patch_index = lax.axis_index("patch")
    first_pair = lax.axis_index("seq") * pairs_here
    seq_len = stale_kv.shape[1]
    text_len = TXT_DEV * seq_len // (TXT_DEV + IMG_DEV)
    image_index = (first_pair + jnp.arange(pairs_here)) // HEADS
    matches = image_index[:, None] == jnp.arange(text_count.shape[0])[None, :]
    valid_counts = jnp.sum(jnp.where(matches, text_count[None, :], 0), axis=1)
    halves = seq_count % 2 == 0 and patch_len % 16 == 0
    if pairs_here % PAIR_TILE == 0 and halves and lax.axis_size("patch") == 4:
        return fused(fresh_qkv, stale_kv, text_count, text_len)
    exchanged = lax.all_to_all(fresh_qkv, "seq", split_axis=2, concat_axis=1, tiled=True)
    query_part = exchanged[0]
    own_kv = exchanged[1:]
    refreshed = lax.all_gather(own_kv, "patch", axis=1, tiled=True)
    merged_kv = lax.dynamic_update_slice_in_dim(stale_kv, own_kv, patch_index * patch_len, 1)
    attended_part = attend(query_part, merged_kv[0], merged_kv[1], valid_counts, text_len)
    result = lax.all_to_all(attended_part, "seq", split_axis=0, concat_axis=1, tiled=True)
    return (result, refreshed)


def solution(mesh):
    in_specs = (P(None, ("patch", "seq"), None, None), P(None, None, "seq", None), P())
    out_specs = (P(("patch", "seq"), None, None), P(None, None, "seq", None))
    return jax.shard_map(
        per_device, mesh=mesh, in_specs=in_specs, out_specs=out_specs, check_vma=False
    )
```

```python
import functools
import math

import jax
import jax.numpy as jnp
from jax import lax
from jax.experimental import pallas as pl
from jax.experimental.pallas import tpu as pltpu
from jax.sharding import PartitionSpec as P

HEADS = 24
TXT_DEV = 2
IMG_DEV = 16
PAIR_TILE = 8
MESH = pl.DeviceIdType.MESH


def fused_kernel(
    text_len,
    counts_ref,
    fresh_ref,
    stale_ref,
    attended_ref,
    refreshed_ref,
    counts,
    recv,
    stale_vmem,
    wide,
    keys,
    values,
    queries,
    out_wide,
    out_send,
    counts_sem,
    in_send_sem,
    in_recv_sem,
    own_sem,
    stale_sem,
    fwd_send_sem,
    fwd_recv_sem,
    keep_sem,
    out_send_sem,
    out_recv_sem,
    out_own_sem,
):
    _, rows, peers, chunks, tile, hdim = fresh_ref.shape
    group_len = rows * peers
    seq_len = stale_ref.shape[1]
    p = lax.axis_index("patch")
    s = lax.axis_index("seq")
    core_twin = p + 1 - 2 * (p % 2)
    x_twin = (p + 2) % 4
    scale = 1.0 / math.sqrt(hdim)

    barrier = pltpu.get_barrier_semaphore()
    for step in range(1, peers):
        pl.semaphore_signal(
            barrier, inc=1, device_id=(p, (s + step) % peers), device_id_type=MESH
        )
    for twin in (core_twin, x_twin):
        pl.semaphore_signal(barrier, inc=1, device_id=(twin, s), device_id_type=MESH)

    counts_copy = pltpu.make_async_copy(counts_ref, counts, counts_sem.at[0])
    counts_copy.start()
    stale_copies = []
    for c in range(chunks):
        for which in range(2):
            copy = pltpu.make_async_copy(
                stale_ref.at[which, :, c], stale_vmem.at[which, c], stale_sem.at[which, c]
            )
            copy.start()
            stale_copies.append(copy)
    own_copies = []
    for c in range(chunks):
        copy = pltpu.make_async_copy(
            fresh_ref.at[:, :, s, c], recv.at[c, :, pl.ds(rows * s, rows)], own_sem.at[c]
        )
        copy.start()
        own_copies.append(copy)
    pl.semaphore_wait(barrier, peers + 1)

    groups = [(0, 1, 2), (0, 0, 1)]
    groups += [(c, 1, 2) for c in range(1, chunks)]
    groups += [(c, 0, 1) for c in range(1, chunks)]

    def in_copy(k, step):
        c, first, count = groups[k]
        to = (s + step) % peers
        return pltpu.make_async_remote_copy(
            src_ref=fresh_ref.at[pl.ds(first, count), :, to, c],
            dst_ref=recv.at[c, pl.ds(first, count), pl.ds(rows * s, rows)],
            send_sem=in_send_sem.at[k, step],
            recv_sem=in_recv_sem.at[k, step],
            device_id=(p, to),
            device_id_type=MESH,
        )

    def in_arrival(k, step):
        c, first, count = groups[k]
        origin = (s + peers - step) % peers
        return pltpu.make_async_remote_copy(
            src_ref=fresh_ref.at[pl.ds(first, count), :, origin, c],
            dst_ref=recv.at[c, pl.ds(first, count), pl.ds(rows * origin, rows)],
            send_sem=in_send_sem.at[k, step],
            recv_sem=in_recv_sem.at[k, step],
            device_id=(p, origin),
            device_id_type=MESH,
        )

    def forward(c, kind):
        if kind == 2:
            place = refreshed_ref.at[:, pl.ds(group_len * x_twin, group_len), c]
            source = place
        else:
            place = refreshed_ref.at[:, pl.ds(group_len * p, group_len), c]
            source = recv.at[c, pl.ds(1, 2)]
        return pltpu.make_async_remote_copy(
            src_ref=source,
            dst_ref=place,
            send_sem=fwd_send_sem.at[kind, c],
            recv_sem=fwd_recv_sem.at[kind, c],
            device_id=(x_twin if kind == 0 else core_twin, s),
            device_id_type=MESH,
        )

    def forward_arrival(c, kind):
        origin = {0: x_twin, 1: core_twin, 2: (core_twin + 2) % 4}[kind]
        return pltpu.make_async_remote_copy(
            src_ref=recv.at[c, pl.ds(1, 2)],
            dst_ref=refreshed_ref.at[:, pl.ds(group_len * origin, group_len), c],
            send_sem=fwd_send_sem.at[kind, c],
            recv_sem=fwd_recv_sem.at[kind, c],
            device_id=(x_twin if kind == 0 else core_twin, s),
            device_id_type=MESH,
        )

    def keep(c):
        return pltpu.make_async_copy(
            recv.at[c, pl.ds(1, 2)],
            refreshed_ref.at[:, pl.ds(group_len * p, group_len), c],
            keep_sem.at[c],
        )

    def out_copy(c, step):
        to = (s + step) % peers
        return pltpu.make_async_remote_copy(
            src_ref=out_send.at[c, pl.ds(rows * to, rows)],
            dst_ref=attended_ref.at[:, s, c],
            send_sem=out_send_sem.at[c, step],
            recv_sem=out_recv_sem.at[c, step],
            device_id=(p, to),
            device_id_type=MESH,
        )

    def out_arrival(c, step):
        origin = (s + peers - step) % peers
        return pltpu.make_async_remote_copy(
            src_ref=out_send.at[c, pl.ds(rows * origin, rows)],
            dst_ref=attended_ref.at[:, origin, c],
            send_sem=out_send_sem.at[c, step],
            recv_sem=out_recv_sem.at[c, step],
            device_id=(p, origin),
            device_id_type=MESH,
        )

    def out_own(c):
        return pltpu.make_async_copy(
            out_send.at[c, pl.ds(rows * s, rows)], attended_ref.at[:, s, c], out_own_sem.at[c]
        )

    last = len(groups) - 1

    def follow(k):
        after = k + 1 if k == last - 1 else k + 2
        for step in range(1, peers):
            in_copy(k, step).wait_send()
            if after < last or after == k + 1:
                in_copy(after, step).start()

    for k in range(min(2, last)):
        for step in range(1, peers):
            in_copy(k, step).start()

    counts_copy.wait()
    for copy in stale_copies:
        copy.wait()
    for c in range(chunks):
        for which, target in ((0, keys), (1, values)):
            wide[...] = stale_vmem[which, c].astype(jnp.float32).reshape(seq_len * tile, hdim)
            for g in range(tile):
                target[c * tile + g] = wide[pl.ds(g, seq_len, stride=tile), :].astype(jnp.bfloat16)

    masked_lanes = min(seq_len, -(-text_len // 128) * 128)
    position = lax.broadcasted_iota(jnp.int32, (1, masked_lanes), 1)

    def rows_of_pairs(c, which):
        part = wide.at[pl.ds(0, group_len * tile)]
        part[...] = recv[c, which].astype(jnp.float32).reshape(group_len * tile, hdim)
        return [
            part[pl.ds(g, group_len, stride=tile), :].astype(jnp.bfloat16) for g in range(tile)
        ]

    def send_keys(c):
        forward(c, 0).start()
        forward(c, 1).start()
        keep(c).start()

    def store_keys(c):
        place = pl.ds(pl.multiple_of(group_len * p, 16), group_len)
        for which, target in ((1, keys), (2, values)):
            for g, block in enumerate(rows_of_pairs(c, which)):
                target[c * tile + g, place, :] = block

    def attend_chunk(c):
        for g, query in enumerate(rows_of_pairs(c, 0)):
            queries[g] = query
        for g in range(tile):
            pair = c * tile + g
            scores = lax.dot_general(
                queries[g], keys[pair], (((1,), (1,)), ((), ())), preferred_element_type=jnp.float32
            )
            image = (s * (chunks * tile) + pair) // HEADS
            visible = (position >= text_len) | (position < counts[image])
            text_scores = jnp.where(visible, scores[:, :masked_lanes], -jnp.inf)
            if masked_lanes < seq_len:
                scores = jnp.concatenate([text_scores, scores[:, masked_lanes:]], axis=1)
            else:
                scores = text_scores
            highest = jnp.max(scores, axis=1, keepdims=True)
            raised = jnp.exp2((scores - highest) * (scale * math.log2(math.e)))
            total = jnp.sum(raised, axis=1, keepdims=True)
            weights = (raised * (1.0 / total)).astype(jnp.bfloat16)
            out_wide[pl.ds(g, group_len, stride=tile), :] = jnp.dot(
                weights, values[pair], preferred_element_type=jnp.float32
            )
        out_send[c] = out_wide[...].reshape(group_len, tile, hdim).astype(jnp.bfloat16)
        for step in range(1, peers):
            out_copy(c, step).start()
        out_own(c).start()

    relays = 0
    followed = []
    for copy in own_copies:
        copy.wait()
    for k, (c, first, _) in enumerate(groups):
        if k not in followed:
            follow(k)
        for step in range(1, peers):
            in_arrival(k, step).wait_recv()
        if first == 1:
            send_keys(c)
            if k == last - 2:
                follow(k + 1)
                followed.append(k + 1)
            store_keys(c)
        else:
            attend_chunk(c)
        if k >= 2 and relays + 1 < chunks:
            forward_arrival(relays, 0).wait_recv()
            forward(relays, 2).start()
            relays += 1

    forward_arrival(chunks - 1, 0).wait_recv()
    forward(chunks - 1, 2).start()
    for c in range(chunks):
        for step in range(1, peers):
            out_copy(c, step).wait_send()
            out_arrival(c, step).wait_recv()
        out_own(c).wait()
        keep(c).wait()
        forward(c, 0).wait_send()
        for kind in (1, 2):
            forward(c, kind).wait_send()
            forward_arrival(c, kind).wait_recv()


def fused(fresh_qkv, stale_kv, text_count, text_len):
    peers = lax.axis_size("seq")
    _, rows, pair_count, hdim = fresh_qkv.shape
    pairs_here = pair_count // peers
    chunks = pairs_here // PAIR_TILE
    group_len = rows * peers
    seq_len = stale_kv.shape[1]
    bf16, f32 = jnp.bfloat16, jnp.float32
    fresh_blocks = fresh_qkv.reshape(3, rows, peers, chunks, PAIR_TILE, hdim)
    stale_blocks = stale_kv.reshape(2, seq_len, chunks, PAIR_TILE, hdim)
    attended_shape = (rows, peers, chunks, PAIR_TILE, hdim)
    dma = pltpu.SemaphoreType.DMA
    in_hbm = pl.BlockSpec(memory_space=pltpu.HBM)
    anywhere = pl.BlockSpec(memory_space=pl.ANY)
    attended, refreshed = pl.pallas_call(
        functools.partial(fused_kernel, text_len),
        out_shape=(
            pltpu.VMEM(attended_shape, bf16),
            pltpu.VMEM(stale_blocks.shape, bf16),
        ),
        in_specs=[in_hbm, in_hbm, in_hbm],
        out_specs=(anywhere, anywhere),
        scratch_shapes=[
            pltpu.SMEM(text_count.shape, jnp.int32),
            pltpu.VMEM((chunks, 3, group_len, PAIR_TILE, hdim), bf16),
            pltpu.VMEM((2, chunks, seq_len, PAIR_TILE, hdim), bf16),
            pltpu.VMEM((seq_len * PAIR_TILE, hdim), f32),
            pltpu.VMEM((pairs_here, seq_len, hdim), bf16),
            pltpu.VMEM((pairs_here, seq_len, hdim), bf16),
            pltpu.VMEM((PAIR_TILE, group_len, hdim), bf16),
            pltpu.VMEM((group_len * PAIR_TILE, hdim), f32),
            pltpu.VMEM((chunks, group_len, PAIR_TILE, hdim), bf16),
            dma((1,)),
            dma((2 * chunks, peers)),
            dma((2 * chunks, peers)),
            dma((chunks,)),
            dma((2, chunks)),
            dma((3, chunks)),
            dma((3, chunks)),
            dma((chunks,)),
            dma((chunks, peers)),
            dma((chunks, peers)),
            dma((chunks,)),
        ],
        compiler_params=pltpu.CompilerParams(
            collective_id=0, has_side_effects=True, vmem_limit_bytes=32 * 1024 * 1024
        ),
        name="joint_attention",
    )(
        pltpu.with_memory_space_constraint(text_count, pltpu.HBM),
        pltpu.with_memory_space_constraint(fresh_blocks, pltpu.HBM),
        pltpu.with_memory_space_constraint(stale_blocks, pltpu.HBM),
    )
    return attended.reshape(rows, pair_count, hdim), refreshed.reshape(stale_kv.shape)


def attend(query_part, key_part, value_part, valid_counts, text_len):
    score_scale = 1.0 / math.sqrt(query_part.shape[-1])
    position = jnp.arange(key_part.shape[0])

    def per_pair(operands):
        query_rows, key_rows, value_rows, valid_text = operands
        scores = (
            lax.dot_general(
                query_rows, key_rows, (((1,), (1,)), ((), ())), preferred_element_type=jnp.float32
            )
            * score_scale
        )
        visible = (position >= text_len) | (position < valid_text)
        scores = jnp.where(visible[None, :], scores, -jnp.inf)
        highest = jnp.max(scores, axis=1, keepdims=True)
        raised = jnp.exp(scores - highest)
        weights = (raised / jnp.sum(raised, axis=1, keepdims=True)).astype(jnp.bfloat16)
        return jnp.dot(weights, value_rows, preferred_element_type=jnp.float32).astype(jnp.bfloat16)

    outputs = lax.map(
        per_pair,
        (
            jnp.moveaxis(query_part, 1, 0),
            jnp.moveaxis(key_part, 1, 0),
            jnp.moveaxis(value_part, 1, 0),
            valid_counts,
        ),
    )
    return jnp.moveaxis(outputs, 0, 1)


def per_device(fresh_qkv, stale_kv, text_count):
    seq_count = lax.axis_size("seq")
    shard_rows = fresh_qkv.shape[1]
    pairs_here = fresh_qkv.shape[2] // seq_count
    patch_len = shard_rows * seq_count
    patch_index = lax.axis_index("patch")
    first_pair = lax.axis_index("seq") * pairs_here
    seq_len = stale_kv.shape[1]
    text_len = TXT_DEV * seq_len // (TXT_DEV + IMG_DEV)
    image_index = (first_pair + jnp.arange(pairs_here)) // HEADS
    matches = image_index[:, None] == jnp.arange(text_count.shape[0])[None, :]
    valid_counts = jnp.sum(jnp.where(matches, text_count[None, :], 0), axis=1)
    if pairs_here % PAIR_TILE == 0 and patch_len % 16 == 0 and lax.axis_size("patch") == 4:
        return fused(fresh_qkv, stale_kv, text_count, text_len)
    exchanged = lax.all_to_all(fresh_qkv, "seq", split_axis=2, concat_axis=1, tiled=True)
    query_part = exchanged[0]
    own_kv = exchanged[1:]
    refreshed = lax.all_gather(own_kv, "patch", axis=1, tiled=True)
    merged_kv = lax.dynamic_update_slice_in_dim(stale_kv, own_kv, patch_index * patch_len, 1)
    attended_part = attend(query_part, merged_kv[0], merged_kv[1], valid_counts, text_len)
    result = lax.all_to_all(attended_part, "seq", split_axis=0, concat_axis=1, tiled=True)
    return (result, refreshed)


def solution(mesh):
    in_specs = (P(None, ("patch", "seq"), None, None), P(None, None, "seq", None), P())
    out_specs = (P(("patch", "seq"), None, None), P(None, None, "seq", None))
    return jax.shard_map(
        per_device, mesh=mesh, in_specs=in_specs, out_specs=out_specs, check_vma=False
    )
```

```python
import functools
import math

import jax
import jax.numpy as jnp
from jax import lax
from jax.experimental import pallas as pl
from jax.experimental.pallas import tpu as pltpu
from jax.sharding import PartitionSpec as P

HEADS = 24
TXT_DEV = 2
IMG_DEV = 16
PAIR_TILE = 8
MESH = pl.DeviceIdType.MESH


def fused_kernel(
    text_len,
    counts_ref,
    fresh_ref,
    stale_ref,
    attended_ref,
    refreshed_ref,
    counts,
    recv,
    stale_vmem,
    wide,
    keys,
    values,
    queries,
    out_wide,
    out_send,
    counts_sem,
    in_send_sem,
    in_recv_sem,
    own_sem,
    stale_sem,
    fwd_send_sem,
    fwd_recv_sem,
    keep_sem,
    out_send_sem,
    out_recv_sem,
    out_own_sem,
):
    _, rows, peers, chunks, tile, hdim = fresh_ref.shape
    group_len = rows * peers
    seq_len = stale_ref.shape[1]
    p = lax.axis_index("patch")
    s = lax.axis_index("seq")
    core_twin = p + 1 - 2 * (p % 2)
    x_twin = (p + 2) % 4
    scale = 1.0 / math.sqrt(hdim)

    barrier = pltpu.get_barrier_semaphore()
    for step in range(1, peers):
        pl.semaphore_signal(
            barrier, inc=1, device_id=(p, (s + step) % peers), device_id_type=MESH
        )
    for twin in (core_twin, x_twin):
        pl.semaphore_signal(barrier, inc=1, device_id=(twin, s), device_id_type=MESH)

    pl.semaphore_wait(barrier, peers + 1)

    groups = [(c, 1, 2) for c in range(chunks)] + [(c, 0, 1) for c in range(chunks)]

    def in_copy(k, step):
        c, first, count = groups[k]
        to = (s + step) % peers
        return pltpu.make_async_remote_copy(
            src_ref=fresh_ref.at[pl.ds(first, count), :, to, c],
            dst_ref=recv.at[c, pl.ds(first, count), pl.ds(rows * s, rows)],
            send_sem=in_send_sem.at[k, step],
            recv_sem=in_recv_sem.at[k, step],
            device_id=(p, to),
            device_id_type=MESH,
        )

    def in_arrival(k, step):
        c, first, count = groups[k]
        origin = (s + peers - step) % peers
        return pltpu.make_async_remote_copy(
            src_ref=fresh_ref.at[pl.ds(first, count), :, origin, c],
            dst_ref=recv.at[c, pl.ds(first, count), pl.ds(rows * origin, rows)],
            send_sem=in_send_sem.at[k, step],
            recv_sem=in_recv_sem.at[k, step],
            device_id=(p, origin),
            device_id_type=MESH,
        )

    def forward(c, kind):
        if kind == 2:
            place = refreshed_ref.at[:, pl.ds(group_len * x_twin, group_len), c]
            source = place
        else:
            place = refreshed_ref.at[:, pl.ds(group_len * p, group_len), c]
            source = recv.at[c, pl.ds(1, 2)]
        return pltpu.make_async_remote_copy(
            src_ref=source,
            dst_ref=place,
            send_sem=fwd_send_sem.at[kind, c],
            recv_sem=fwd_recv_sem.at[kind, c],
            device_id=(x_twin if kind == 0 else core_twin, s),
            device_id_type=MESH,
        )

    def forward_arrival(c, kind):
        origin = {0: x_twin, 1: core_twin, 2: (core_twin + 2) % 4}[kind]
        return pltpu.make_async_remote_copy(
            src_ref=recv.at[c, pl.ds(1, 2)],
            dst_ref=refreshed_ref.at[:, pl.ds(group_len * origin, group_len), c],
            send_sem=fwd_send_sem.at[kind, c],
            recv_sem=fwd_recv_sem.at[kind, c],
            device_id=(x_twin if kind == 0 else core_twin, s),
            device_id_type=MESH,
        )

    def keep(c):
        return pltpu.make_async_copy(
            recv.at[c, pl.ds(1, 2)],
            refreshed_ref.at[:, pl.ds(group_len * p, group_len), c],
            keep_sem.at[c],
        )

    def out_copy(c, step):
        to = (s + step) % peers
        return pltpu.make_async_remote_copy(
            src_ref=out_send.at[c, pl.ds(rows * to, rows)],
            dst_ref=attended_ref.at[:, s, c],
            send_sem=out_send_sem.at[c, step],
            recv_sem=out_recv_sem.at[c, step],
            device_id=(p, to),
            device_id_type=MESH,
        )

    def out_arrival(c, step):
        origin = (s + peers - step) % peers
        return pltpu.make_async_remote_copy(
            src_ref=out_send.at[c, pl.ds(rows * origin, rows)],
            dst_ref=attended_ref.at[:, origin, c],
            send_sem=out_send_sem.at[c, step],
            recv_sem=out_recv_sem.at[c, step],
            device_id=(p, origin),
            device_id_type=MESH,
        )

    def out_own(c):
        return pltpu.make_async_copy(
            out_send.at[c, pl.ds(rows * s, rows)], attended_ref.at[:, s, c], out_own_sem.at[c]
        )

    def follow(k):
        for step in range(1, peers):
            in_copy(k, step).wait_send()
            if k + 2 < len(groups):
                in_copy(k + 2, step).start()

    for k in range(2):
        for step in range(1, peers):
            in_copy(k, step).start()

    counts_copy = pltpu.make_async_copy(counts_ref, counts, counts_sem.at[0])
    counts_copy.start()
    stale_copies = []
    for c in range(chunks):
        for which in range(2):
            copy = pltpu.make_async_copy(
                stale_ref.at[which, :, c], stale_vmem.at[which, c], stale_sem.at[which, c]
            )
            copy.start()
            stale_copies.append(copy)
    own_copies = []
    for c in range(chunks):
        copy = pltpu.make_async_copy(
            fresh_ref.at[:, :, s, c], recv.at[c, :, pl.ds(rows * s, rows)], own_sem.at[c]
        )
        copy.start()
        own_copies.append(copy)
    masked_lanes = min(seq_len, -(-text_len // 128) * 128)
    position = lax.broadcasted_iota(jnp.int32, (1, masked_lanes), 1)

    def rows_of_pairs(c, which):
        part = wide.at[pl.ds(0, group_len * tile)]
        part[...] = recv[c, which].astype(jnp.float32).reshape(group_len * tile, hdim)
        return [
            part[pl.ds(g, group_len, stride=tile), :].astype(jnp.bfloat16) for g in range(tile)
        ]

    def send_keys(c):
        forward(c, 0).start()
        forward(c, 1).start()
        keep(c).start()

    def store_keys(c):
        place = pl.ds(pl.multiple_of(group_len * p, 16), group_len)
        for which, target in ((1, keys), (2, values)):
            stale_copies[2 * c + which - 1].wait()
            block = stale_vmem[which - 1, c].astype(jnp.float32)
            wide[...] = block.reshape(seq_len * tile, hdim)
            for g in range(tile):
                target[c * tile + g] = wide[pl.ds(g, seq_len, stride=tile), :].astype(jnp.bfloat16)
            for g, block in enumerate(rows_of_pairs(c, which)):
                target[c * tile + g, place, :] = block

    def attend_chunk(c):
        for g, query in enumerate(rows_of_pairs(c, 0)):
            queries[g] = query
        for g in range(tile):
            pair = c * tile + g
            scores = lax.dot_general(
                queries[g], keys[pair], (((1,), (1,)), ((), ())), preferred_element_type=jnp.float32
            )
            image = (s * (chunks * tile) + pair) // HEADS
            visible = (position >= text_len) | (position < counts[image])
            text_scores = jnp.where(visible, scores[:, :masked_lanes], -jnp.inf)
            if masked_lanes < seq_len:
                scores = jnp.concatenate([text_scores, scores[:, masked_lanes:]], axis=1)
            else:
                scores = text_scores
            highest = jnp.max(scores, axis=1, keepdims=True)
            raised = jnp.exp2((scores - highest) * (scale * math.log2(math.e)))
            total = jnp.sum(raised, axis=1, keepdims=True)
            weights = (raised * (1.0 / total)).astype(jnp.bfloat16)
            out_wide[pl.ds(g, group_len, stride=tile), :] = jnp.dot(
                weights, values[pair], preferred_element_type=jnp.float32
            )
        out_send[c] = out_wide[...].reshape(group_len, tile, hdim).astype(jnp.bfloat16)
        for step in range(1, peers):
            out_copy(c, step).start()
        out_own(c).start()

    def relay(c):
        forward_arrival(c, 0).wait_recv()
        forward(c, 2).start()

    counts_copy.wait()
    for copy in own_copies:
        copy.wait()
    for k, (c, first, _) in enumerate(groups):
        follow(k)
        for step in range(1, peers):
            in_arrival(k, step).wait_recv()
        if first == 1:
            send_keys(c)
            store_keys(c)
            if c:
                relay(c - 1)
        else:
            attend_chunk(c)
            if c == max(chunks - 2, 0):
                relay(chunks - 1)

    for c in range(chunks):
        for step in range(1, peers):
            out_copy(c, step).wait_send()
            out_arrival(c, step).wait_recv()
        out_own(c).wait()
        keep(c).wait()
        forward(c, 0).wait_send()
        for kind in (1, 2):
            forward(c, kind).wait_send()
            forward_arrival(c, kind).wait_recv()


def fused(fresh_qkv, stale_kv, text_count, text_len):
    peers = lax.axis_size("seq")
    _, rows, pair_count, hdim = fresh_qkv.shape
    pairs_here = pair_count // peers
    chunks = pairs_here // PAIR_TILE
    group_len = rows * peers
    seq_len = stale_kv.shape[1]
    bf16, f32 = jnp.bfloat16, jnp.float32
    fresh_blocks = fresh_qkv.reshape(3, rows, peers, chunks, PAIR_TILE, hdim)
    stale_blocks = stale_kv.reshape(2, seq_len, chunks, PAIR_TILE, hdim)
    attended_shape = (rows, peers, chunks, PAIR_TILE, hdim)
    dma = pltpu.SemaphoreType.DMA
    in_hbm = pl.BlockSpec(memory_space=pltpu.HBM)
    anywhere = pl.BlockSpec(memory_space=pl.ANY)
    attended, refreshed = pl.pallas_call(
        functools.partial(fused_kernel, text_len),
        out_shape=(
            pltpu.VMEM(attended_shape, bf16),
            pltpu.VMEM(stale_blocks.shape, bf16),
        ),
        in_specs=[in_hbm, in_hbm, in_hbm],
        out_specs=(anywhere, anywhere),
        scratch_shapes=[
            pltpu.SMEM(text_count.shape, jnp.int32),
            pltpu.VMEM((chunks, 3, group_len, PAIR_TILE, hdim), bf16),
            pltpu.VMEM((2, chunks, seq_len, PAIR_TILE, hdim), bf16),
            pltpu.VMEM((seq_len * PAIR_TILE, hdim), f32),
            pltpu.VMEM((pairs_here, seq_len, hdim), bf16),
            pltpu.VMEM((pairs_here, seq_len, hdim), bf16),
            pltpu.VMEM((PAIR_TILE, group_len, hdim), bf16),
            pltpu.VMEM((group_len * PAIR_TILE, hdim), f32),
            pltpu.VMEM((chunks, group_len, PAIR_TILE, hdim), bf16),
            dma((1,)),
            dma((2 * chunks, peers)),
            dma((2 * chunks, peers)),
            dma((chunks,)),
            dma((2, chunks)),
            dma((3, chunks)),
            dma((3, chunks)),
            dma((chunks,)),
            dma((chunks, peers)),
            dma((chunks, peers)),
            dma((chunks,)),
        ],
        compiler_params=pltpu.CompilerParams(
            collective_id=0, has_side_effects=True, vmem_limit_bytes=32 * 1024 * 1024
        ),
        name="joint_attention",
    )(
        pltpu.with_memory_space_constraint(text_count, pltpu.HBM),
        pltpu.with_memory_space_constraint(fresh_blocks, pltpu.HBM),
        pltpu.with_memory_space_constraint(stale_blocks, pltpu.HBM),
    )
    return attended.reshape(rows, pair_count, hdim), refreshed.reshape(stale_kv.shape)


def attend(query_part, key_part, value_part, valid_counts, text_len):
    score_scale = 1.0 / math.sqrt(query_part.shape[-1])
    position = jnp.arange(key_part.shape[0])

    def per_pair(operands):
        query_rows, key_rows, value_rows, valid_text = operands
        scores = (
            lax.dot_general(
                query_rows, key_rows, (((1,), (1,)), ((), ())), preferred_element_type=jnp.float32
            )
            * score_scale
        )
        visible = (position >= text_len) | (position < valid_text)
        scores = jnp.where(visible[None, :], scores, -jnp.inf)
        highest = jnp.max(scores, axis=1, keepdims=True)
        raised = jnp.exp(scores - highest)
        weights = (raised / jnp.sum(raised, axis=1, keepdims=True)).astype(jnp.bfloat16)
        return jnp.dot(weights, value_rows, preferred_element_type=jnp.float32).astype(jnp.bfloat16)

    outputs = lax.map(
        per_pair,
        (
            jnp.moveaxis(query_part, 1, 0),
            jnp.moveaxis(key_part, 1, 0),
            jnp.moveaxis(value_part, 1, 0),
            valid_counts,
        ),
    )
    return jnp.moveaxis(outputs, 0, 1)


def per_device(fresh_qkv, stale_kv, text_count):
    seq_count = lax.axis_size("seq")
    shard_rows = fresh_qkv.shape[1]
    pairs_here = fresh_qkv.shape[2] // seq_count
    patch_len = shard_rows * seq_count
    patch_index = lax.axis_index("patch")
    first_pair = lax.axis_index("seq") * pairs_here
    seq_len = stale_kv.shape[1]
    text_len = TXT_DEV * seq_len // (TXT_DEV + IMG_DEV)
    image_index = (first_pair + jnp.arange(pairs_here)) // HEADS
    matches = image_index[:, None] == jnp.arange(text_count.shape[0])[None, :]
    valid_counts = jnp.sum(jnp.where(matches, text_count[None, :], 0), axis=1)
    if pairs_here % PAIR_TILE == 0 and patch_len % 16 == 0 and lax.axis_size("patch") == 4:
        return fused(fresh_qkv, stale_kv, text_count, text_len)
    exchanged = lax.all_to_all(fresh_qkv, "seq", split_axis=2, concat_axis=1, tiled=True)
    query_part = exchanged[0]
    own_kv = exchanged[1:]
    refreshed = lax.all_gather(own_kv, "patch", axis=1, tiled=True)
    merged_kv = lax.dynamic_update_slice_in_dim(stale_kv, own_kv, patch_index * patch_len, 1)
    attended_part = attend(query_part, merged_kv[0], merged_kv[1], valid_counts, text_len)
    result = lax.all_to_all(attended_part, "seq", split_axis=0, concat_axis=1, tiled=True)
    return (result, refreshed)


def solution(mesh):
    in_specs = (P(None, ("patch", "seq"), None, None), P(None, None, "seq", None), P())
    out_specs = (P(("patch", "seq"), None, None), P(None, None, "seq", None))
    return jax.shard_map(
        per_device, mesh=mesh, in_specs=in_specs, out_specs=out_specs, check_vma=False
    )
```
